32 devices in a mesh: expert: 16 (over z, y, x), dp: 2 (over core).
Axes of the slice: x: 2, y: 2, z: 4, core: 2. Of those that a mesh axis runs over, the one named last changes fastest.
Arguments:
- tokens: bfloat16 [2048, 3584], P('expert'), may hold values from -6 to 6
- expert_ids: int32 [2048, 8], P('expert'), may hold values from 0 to 15, all different within a row; in each aligned block of 128 rows (0 to 127, 128 to 255, ...) at most 96 rows name the same one
- route_weights: float32 [2048, 8], P('expert'), may hold values from 0.05 to 0.45
- gate_up_panels: bfloat16 [16, 2, 1792, 2048], P('expert', 'dp'), may hold values from -0.09375 to 0.09375
- down_panels: bfloat16 [16, 1024, 3584], P('expert', None, 'dp'), may hold values from -0.1875 to 0.1875
- partner: int32 [16], replicated, may hold values from 0 to 15, as said below
Outputs:
- moe_out: bfloat16 [2048, 3584], P('expert', 'dp')
- new_gate_up: bfloat16 [16, 2, 1792, 2048], P('expert', 'dp')
- new_down: bfloat16 [16, 1024, 3584], P('expert', None, 'dp')
The draws below stay inside these ranges and needn't reach their ends.
Inputs may be any that keep to these rules, and one draw needn't show every extreme that they name: `expert_ids`: in the 128 rows of one index of the expert axis, each row names 8 different experts and no expert is named by more than 96 rows. partner[i] is i, i XOR 1 or i XOR 2, the same of these for the four indices of each aligned group of four; partner[partner[i]] = i; some group takes XOR 1 and some group XOR 2.
All inputs are finite; a program needn't handle non-finite values.
Results may differ from the reference program's by a relative error of at most 0.0057.
Values may be sent and summed in bfloat16 or wider, within the bound.
A program may use at most 128 MiB of HBM per device.

```python
import math
import jax
import jax.numpy as jnp
import numpy as np
from jax import lax

D = 3584
FF = 1024
TOP = 8
TOK = 128
EXPERTS = 16
TOKENS = 2048
CAP = 96
HID = 1024
N_EXPERT = 16
N_DP = 2


def draw_partner(key, part):
    group_count = EXPERTS // 4
    first_key, second_key = jax.random.split(jax.random.fold_in(key, 17))
    kinds = jax.random.randint(first_key, (group_count,), 0, 3)
    order = jax.random.permutation(second_key, group_count)
    kinds = kinds.at[order[0]].set(0).at[order[1]].set(1)
    masks = jnp.array([1, 2, 0], dtype=jnp.int32)[kinds]
    indices = jnp.arange(EXPERTS, dtype=jnp.int32)
    return jnp.bitwise_xor(indices, jnp.repeat(masks, 4)).astype(jnp.int32)


def level_of(rng, dims, pieces, smallest, largest):
    gain, own = 1.0, jax.random.fold_in(rng, 6)
    for axis_at, shards_of in pieces:
        heights = jnp.exp(jax.random.uniform(jax.random.fold_in(own, axis_at), (shards_of,), jnp.float32, smallest / len(pieces), largest / len(pieces)))
        gain = gain * jnp.repeat(heights, dims[axis_at] // shards_of).reshape([-1 if axis == axis_at else 1 for axis in range(len(dims))])
    return gain


def deal_out(stream_key, own, number, rows, count, top, most, slope):
    ranking = jax.random.permutation(stream_key, count)
    heavy_load, ordinary = shares(count, rows * top, most, slope, True), shares(count, rows * top, most, slope, False)
    places = jnp.arange(count)

    def named(sizes, offset_by):
        used = int((sizes > 0).sum())
        fixed = max(1, used // 4)
        passed = fixed + (places - fixed + offset_by * (used - fixed)) % max(1, count - fixed)
        return jnp.zeros((count,), jnp.int32).at[ranking[jnp.where(places < fixed, places, passed)]].set(jnp.asarray(sizes, jnp.int32))

    sizes = jnp.where(number % 4 == 0, named(heavy_load, number // 4), named(ordinary, number - number // 4 - 1))
    mixed = jax.random.permutation(jax.random.fold_in(own, 3), count)
    giver, sink = mixed[0:count // 2 * 2:2], mixed[1:count // 2 * 2:2]
    room = jnp.minimum(sizes[giver] - 1, most - sizes[sink]) // 2
    room = jnp.where((giver == ranking[0]) | (sink == ranking[0]) | (sizes[sink] == 0), 0, jnp.maximum(room, 0))
    passed = jax.random.randint(jax.random.fold_in(own, 4), (count // 2,), 0, 1 << 20) % (room + 1)
    sizes = sizes.at[giver].add(-passed).at[sink].add(passed)
    members = jnp.searchsorted(jnp.cumsum(sizes), jnp.arange(rows * top), side="right").astype(jnp.int32)
    listing = members.reshape(top, rows).T
    listing = listing[jax.random.permutation(jax.random.fold_in(own, 1), rows)]
    offset_by = jax.random.randint(jax.random.fold_in(own, 2), (rows, 1), 0, top)
    return jnp.take_along_axis(listing, (jnp.arange(top)[None, :] + offset_by) % top, axis=1)


def shares(count, total, limit, skew, full):
    portions = [(1 << 20) // math.isqrt(rank ** skew) + 1 for rank in range(1, count + 1)]
    largest = limit if full else min(limit, max(-(-total // count), total * portions[0] // sum(portions)))
    least = 1 if total - largest >= count - 1 else 0
    counts, spare = [largest] + [least] * (count - 1), total - largest - least * (count - 1)
    while spare > 0:
        movable = [i for i in range(1, count) if counts[i] < largest] or [i for i in range(1, count) if counts[i] < limit]
        whole, budget = sum([portions[i] for i in movable]), spare
        for i in movable:
            more = min(limit - counts[i], max(1, budget * portions[i] // whole), spare)
            counts[i] = counts[i] + more
            spare = spare - more
    return np.array(counts)


def bell_draw(stream_key, shape, width, limit, cuts=(), kind=jnp.bfloat16):
    result = width * jax.random.normal(stream_key, shape, jnp.float32)
    if cuts:
        result = result * level_of(stream_key, shape, cuts, -0.22, 0.18)
    return jnp.clip(result, -limit, limit).astype(kind)


def setup_inputs(seed: int = 0) -> dict:
    key_of = jax.random.split(jax.random.key(seed), 7)
    tokens = bell_draw(key_of[0], (TOKENS, D), 1.0, 6.0, ((0, 16),))
    expert_ids_keys = jax.random.split(jax.random.fold_in(key_of[1], 1), TOKENS // TOK)
    expert_ids_turns = jax.random.permutation(jax.random.fold_in(key_of[1], 3), TOKENS // TOK)
    expert_ids = jax.vmap(lambda own, number: deal_out(jax.random.fold_in(key_of[1], 2), own, number, TOK, EXPERTS, TOP, CAP, 2))(expert_ids_keys, expert_ids_turns).reshape((TOKENS, TOP))
    route_weights = jnp.clip(0.05 + 0.39999999 * jax.random.uniform(key_of[2], (TOKENS, TOP), jnp.float32) ** level_of(key_of[2], (TOKENS, TOP), ((0, 16),), -0.2, 0.2), 0.05, 0.45)
    gate_up_panels = bell_draw(key_of[3], (EXPERTS, N_DP, D // 2, 2 * HID), D ** -0.5, 0.09375, ((0, 16), (1, 2)))
    down_panels = bell_draw(key_of[4], (EXPERTS, FF, D), FF ** -0.5, 0.1875, ((0, 16), (2, 2)))
    partner = draw_partner(jax.random.fold_in(key_of[6], 71), 0)
    return {"tokens": tokens, "expert_ids": expert_ids, "route_weights": route_weights, "gate_up_panels": gate_up_panels, "down_panels": down_panels, "partner": partner}


def unpack_panels(block):
    pair_count = N_DP // 2
    shaped = block.reshape(pair_count, 2, D // 2, 2, HID)
    shaped = jnp.transpose(shaped, (3, 1, 2, 0, 4))
    return shaped.reshape(2, D, FF)


def reference(tokens, expert_ids, route_weights, gate_up_panels, down_panels, partner):
    labels = jnp.arange(EXPERTS, dtype=jnp.int32)
    onehot = (expert_ids[:, :, None] == labels[None, None, :]).astype(jnp.int32)
    picked = jnp.sum(onehot, axis=1).astype(jnp.int32)
    grouped = picked.reshape(N_EXPERT, TOK, EXPERTS)
    slot_rank = (jnp.cumsum(grouped, axis=1).astype(jnp.int32) - grouped).reshape(TOKENS, EXPERTS)
    weight_table = jnp.sum(onehot.astype(jnp.float32) * route_weights[:, :, None], axis=1)
    group_of = (jnp.arange(TOKENS, dtype=jnp.int32) // TOK).astype(jnp.int32)
    padded = jnp.concatenate([tokens, jnp.zeros((1, D), tokens.dtype)], axis=0)
    dummy = N_EXPERT * CAP

    def per_expert(running, expert):
        panels = unpack_panels(lax.dynamic_index_in_dim(gate_up_panels, expert, 0, keepdims=False))
        down = lax.dynamic_index_in_dim(down_panels, expert, 0, keepdims=False)
        column = lax.dynamic_index_in_dim(picked, expert, 1, keepdims=False)
        rank_column = lax.dynamic_index_in_dim(slot_rank, expert, 1, keepdims=False)
        weight_column = lax.dynamic_index_in_dim(weight_table, expert, 1, keepdims=False)
        position = jnp.where(column > 0, group_of * CAP + rank_column, dummy).astype(jnp.int32)
        source = jnp.full((dummy + 1,), TOKENS, jnp.int32).at[position].set(jnp.arange(TOKENS, dtype=jnp.int32))
        buffer = padded[source[:dummy]]
        gate = jnp.dot(buffer, panels[0], preferred_element_type=jnp.float32)
        upward = jnp.dot(buffer, panels[1], preferred_element_type=jnp.float32)
        hidden = (jax.nn.silu(gate) * upward).astype(jnp.bfloat16)
        output = jnp.dot(hidden, down, preferred_element_type=jnp.float32).astype(jnp.bfloat16)
        output = jnp.concatenate([output, jnp.zeros((1, D), output.dtype)], axis=0)
        running = running + weight_column[:, None] * output[position].astype(jnp.float32)
        return running, None

    running, _ = lax.scan(per_expert, jnp.zeros((TOKENS, D), jnp.float32), labels)
    moe_out = running.astype(jnp.bfloat16)
    new_gate_up = jnp.take(gate_up_panels, partner, axis=0)
    new_down = jnp.take(down_panels, partner, axis=0)
    return (moe_out, new_gate_up, new_down)
```

```python
import jax
import jax.numpy as jnp
from jax import lax
from jax.sharding import PartitionSpec as P


def from_partner(block, axis, bit):
    count = lax.axis_size(axis)
    route = []
    for low in range(count):
        high = low | 1 << bit
        if high != low and high < count:
            route += [(low, high), (high, low)]
    return lax.ppermute(block, axis, route)


def pick(own, moved, partner):
    here = lax.axis_index("expert")
    result = own
    for bit_number in range(2):
        taken = partner[here] == jnp.bitwise_xor(here, 1 << bit_number)
        result = jnp.where(taken, moved[bit_number], result)
    return result


def move(block):
    return [from_partner(block, "expert", bit_number) for bit_number in range(2)]


def joined(block):
    if lax.axis_size("dp") > 2:
        return lax.all_gather(block, "dp", axis=1, tiled=True)
    width = block.shape[1]
    side = lax.axis_index("dp")
    other = from_partner(block, "dp", 0)
    first = jnp.where(side == 0, block, other)
    second = jnp.where(side == 0, other, block)
    return jnp.concatenate([first, second], axis=1)


def expert_mlp(flat, gate_up, down, side, moved):
    partial_value = jnp.dot(flat, gate_up, preferred_element_type=jnp.float32)
    half_rows = flat.shape[0] // 2
    mine = lax.dynamic_slice_in_dim(partial_value, side * half_rows, half_rows, 0)
    other = lax.dynamic_slice_in_dim(partial_value, (1 - side) * half_rows, half_rows, 0)
    summed = mine + from_partner(other, "dp", 0)
    block_units = gate_up.shape[1] // 2
    hidden = (jax.nn.silu(summed[:, :block_units]) * summed[:, block_units:]).astype(jnp.bfloat16)
    gathered = joined(hidden)
    gathered, moved = lax.optimization_barrier((gathered, moved))
    pair_count = lax.axis_size("dp") // 2
    out_columns = down.shape[1]
    outputs = jnp.einsum(
        "rqhk,qkc->hrc",
        gathered.reshape(half_rows, pair_count, 2, block_units),
        down.reshape(pair_count, block_units, out_columns),
        preferred_element_type=jnp.float32,
    )
    return outputs.reshape(2 * half_rows, out_columns), moved


def run_layer(tokens, expert_ids, route_weights, gate_up, down, moved):
    devices = lax.axis_size("expert")
    token_rows, model_width = tokens.shape
    top_count = expert_ids.shape[1]
    capacity = min(token_rows, 3 * token_rows * top_count // (2 * devices))
    half_width = model_width // 2
    side = lax.rem(lax.axis_index("dp"), 2)
    own_half = lax.dynamic_slice_in_dim(tokens, side * half_width, half_width, 1)
    labels = jnp.arange(devices, dtype=jnp.int32)
    onehot = (expert_ids[:, :, None] == labels[None, None, :]).astype(jnp.int32)
    picked = jnp.sum(onehot, axis=1)
    earlier = jnp.tri(token_rows, k=-1, dtype=jnp.bfloat16)
    slot_rank = jnp.dot(earlier, picked.astype(jnp.bfloat16), preferred_element_type=jnp.float32).astype(jnp.int32)
    slots = jnp.sum(onehot * slot_rank[:, None, :], axis=2)
    place = (expert_ids * capacity + slots).reshape(-1)
    row_ids = jnp.repeat(jnp.arange(token_rows, dtype=jnp.int32), top_count)
    source = jnp.full((devices * capacity,), token_rows, jnp.int32).at[place].set(row_ids)
    padded = jnp.concatenate([own_half, jnp.zeros((1, half_width), own_half.dtype)], axis=0)
    outgoing = padded[source].reshape(devices, capacity, half_width)
    arrived = lax.all_to_all(outgoing, "expert", split_axis=0, concat_axis=0, tiled=True)
    flat = arrived.reshape(devices * capacity, half_width)
    (early, middle) = moved
    flat, early = lax.optimization_barrier((flat, early))
    outputs, middle = expert_mlp(flat, gate_up, down, side, middle)
    out_columns = down.shape[1]
    expert_out = outputs.reshape(devices, capacity, out_columns).astype(jnp.bfloat16)
    returned = lax.all_to_all(expert_out, "expert", split_axis=0, concat_axis=0, tiled=True)
    chosen = returned.reshape(devices * capacity, out_columns)[place].reshape(
        token_rows, top_count, out_columns
    )
    mixed = jnp.sum(chosen.astype(jnp.float32) * route_weights[:, :, None], axis=1)
    return mixed.astype(jnp.bfloat16), (early, middle)


def per_device(tokens, expert_ids, route_weights, gate_up_panels, down_panels, partner):
    cut = gate_up_panels.shape[2] // 7 * 4
    moe_out, moved = run_layer(
        tokens, expert_ids, route_weights, gate_up_panels[0, 0], down_panels[0], (move(gate_up_panels[:, :, :cut]), move(down_panels))
    )
    late = move(gate_up_panels[:, :, cut:])
    whole = [jnp.concatenate(parts, axis=2) for parts in zip(moved[0], late)]
    new_gate_up = pick(gate_up_panels, whole, partner)
    new_down = pick(down_panels, moved[1], partner)
    return (moe_out, new_gate_up, new_down)


def solution(mesh):
    return jax.shard_map(
        per_device,
        mesh=mesh,
        in_specs=(
            P("expert", None),
            P("expert", None),
            P("expert", None),
            P("expert", "dp", None, None),
            P("expert", None, "dp"),
            P(),
        ),
        out_specs=(P("expert", "dp"), P("expert", "dp", None, None), P("expert", None, "dp")),
        check_vma=False,
    )
```

```python
import jax
import jax.numpy as jnp
from jax import lax
from jax.sharding import PartitionSpec as P


def from_partner(block, axis, bit):
    count = lax.axis_size(axis)
    route = []
    for low in range(count):
        high = low | 1 << bit
        if high != low and high < count:
            route += [(low, high), (high, low)]
    return lax.ppermute(block, axis, route)


def pick(own, moved, partner):
    here = lax.axis_index("expert")
    result = own
    for bit_number in range(2):
        taken = partner[here] == jnp.bitwise_xor(here, 1 << bit_number)
        result = jnp.where(taken, moved[bit_number], result)
    return result


def move(block):
    return [from_partner(block, "expert", bit_number) for bit_number in range(2)]


def tie(value, *moved):
    return lax.optimization_barrier((value, *moved))


def joined(block):
    if lax.axis_size("dp") > 2:
        return lax.all_gather(block, "dp", axis=1, tiled=True)
    width = block.shape[1]
    side = lax.axis_index("dp")
    other = from_partner(block, "dp", 0)
    first = jnp.where(side == 0, block, other)
    second = jnp.where(side == 0, other, block)
    return jnp.concatenate([first, second], axis=1)

def move_parts(block, shares, axis):
    unit = block.shape[axis] // sum(shares)
    parts, start = [], 0
    for share in shares:
        parts.append(move(lax.slice_in_dim(block, start, start + share * unit, axis=axis)))
        start += share * unit
    return parts


def gather_parts(block, parts, partner, axis):
    result, start = block, 0
    for part in parts:
        width = part[0].shape[axis]
        own = lax.slice_in_dim(block, start, start + width, axis=axis)
        result = lax.dynamic_update_slice_in_dim(result, pick(own, part, partner), start, axis)
        start += width
    return result

def expert_mlp(flat, gate_up, down, side, gate_up_parts, down_parts):
    partial_value = jnp.dot(flat, gate_up, preferred_element_type=jnp.float32)
    partial_value, down_parts[0] = tie(partial_value, down_parts[0])
    half_rows = flat.shape[0] // 2
    mine = lax.dynamic_slice_in_dim(partial_value, side * half_rows, half_rows, 0)
    other = lax.dynamic_slice_in_dim(partial_value, (1 - side) * half_rows, half_rows, 0)
    summed = mine + from_partner(other, "dp", 0)
    block_units = gate_up.shape[1] // 2
    hidden = (jax.nn.silu(summed[:, :block_units]) * summed[:, block_units:]).astype(jnp.bfloat16)
    gathered = joined(hidden)
    gathered, down_parts[1] = tie(gathered, down_parts[1])
    pair_count = lax.axis_size("dp") // 2
    out_columns = down.shape[1]
    outputs = jnp.einsum(
        "rqhk,qkc->hrc",
        gathered.reshape(half_rows, pair_count, 2, block_units),
        down.reshape(pair_count, block_units, out_columns),
        preferred_element_type=jnp.float32,
    )
    return outputs.reshape(2 * half_rows, out_columns)


def run_layer(tokens, expert_ids, route_weights, gate_up, down, gate_up_parts, down_parts):
    devices = lax.axis_size("expert")
    token_rows, model_width = tokens.shape
    top_count = expert_ids.shape[1]
    capacity = min(token_rows, 3 * token_rows * top_count // (2 * devices))
    half_width = model_width // 2
    side = lax.rem(lax.axis_index("dp"), 2)
    own_half = lax.dynamic_slice_in_dim(tokens, side * half_width, half_width, 1)
    labels = jnp.arange(devices, dtype=jnp.int32)
    onehot = (expert_ids[:, :, None] == labels[None, None, :]).astype(jnp.int32)
    picked = jnp.sum(onehot, axis=1)
    earlier = jnp.tri(token_rows, k=-1, dtype=jnp.bfloat16)
    slot_rank = jnp.dot(earlier, picked.astype(jnp.bfloat16), preferred_element_type=jnp.float32).astype(jnp.int32)
    slots = jnp.sum(onehot * slot_rank[:, None, :], axis=2)
    place = (expert_ids * capacity + slots).reshape(-1)
    row_ids = jnp.repeat(jnp.arange(token_rows, dtype=jnp.int32), top_count)
    source = jnp.full((devices * capacity,), token_rows, jnp.int32).at[place].set(row_ids)
    padded = jnp.concatenate([own_half, jnp.zeros((1, half_width), own_half.dtype)], axis=0)
    outgoing = padded[source].reshape(devices, capacity, half_width)
    outgoing, gate_up_parts[0] = tie(outgoing, gate_up_parts[0])
    arrived = lax.all_to_all(outgoing, "expert", split_axis=0, concat_axis=0, tiled=True)
    flat = arrived.reshape(devices * capacity, half_width)
    flat, gate_up_parts[1] = tie(flat, gate_up_parts[1])
    outputs = expert_mlp(flat, gate_up, down, side, gate_up_parts, down_parts)
    out_columns = down.shape[1]
    expert_out = outputs.reshape(devices, capacity, out_columns).astype(jnp.bfloat16)
    expert_out, gate_up_parts[2] = tie(expert_out, gate_up_parts[2])
    returned = lax.all_to_all(expert_out, "expert", split_axis=0, concat_axis=0, tiled=True)
    returned, gate_up_parts[3] = tie(returned, gate_up_parts[3])
    chosen = returned.reshape(devices * capacity, out_columns)[place].reshape(
        token_rows, top_count, out_columns
    )
    mixed = jnp.sum(chosen.astype(jnp.float32) * route_weights[:, :, None], axis=1)
    mixed, gate_up_parts[4] = tie(mixed.astype(jnp.bfloat16), gate_up_parts[4])
    return mixed


def per_device(tokens, expert_ids, route_weights, gate_up_panels, down_panels, partner):
    gate_up_parts = move_parts(gate_up_panels, (1, 5, 1, 5, 2), 2)
    down_parts = move_parts(down_panels, (1, 3), 1)
    moe_out = run_layer(
        tokens, expert_ids, route_weights, gate_up_panels[0, 0], down_panels[0], gate_up_parts, down_parts
    )
    new_gate_up = gather_parts(gate_up_panels, gate_up_parts, partner, 2)
    new_down = gather_parts(down_panels, down_parts, partner, 1)
    return (moe_out, new_gate_up, new_down)


def solution(mesh):
    return jax.shard_map(
        per_device,
        mesh=mesh,
        in_specs=(
            P("expert", None),
            P("expert", None),
            P("expert", None),
            P("expert", "dp", None, None),
            P("expert", None, "dp"),
            P(),
        ),
        out_specs=(P("expert", "dp"), P("expert", "dp", None, None), P("expert", None, "dp")),
        check_vma=False,
    )
```
